32 devices in a mesh: region: 4 (over x, core), tm: 8 (over z, y).
Axes of the slice: x: 2, y: 2, z: 4, core: 2. Of those that a mesh axis runs over, the one named last changes fastest.
Arguments:
- waveforms: bfloat16 [3000, 16384], P('region', 'tm'), as said below
- templates: bfloat16 [8, 8, 36, 256], P('tm', None, 'region'), may hold values from -6 to 6
- channel_lists: int32 [8, 8, 36], P(None, None, 'region'), may hold values from 0 to 2999, as said below
- owner_ranks: int32 [2], replicated, may hold values from 0 to 7
Outputs:
- detection: float32 [16, 16384], P(None, 'tm')
The draws below stay inside these ranges and needn't reach their ends.
Inputs may be any that keep to these rules, and one draw needn't show every extreme that they name: `channel_lists`: entry [b, j, c] is a channel of region c // 9: it lies from (c // 9) * 750 to (c // 9 + 1) * 750 - 1. `waveforms`: finite records.
All inputs are finite; a program needn't handle non-finite values.
Results may differ from the reference program's by a relative error of at most 0.0057.
Values may be sent and summed in bfloat16 or wider, within the bound.
A program may use at most 64 MiB of HBM per device.

```python
import math
import jax
import jax.numpy as jnp
from jax import lax

CH_REG = 750
TCH_REG = 9
L = 256
TPB = 8
ROUNDS = 2
CH = 3000
TCH = 36
BLOCKS = 8
NT = 16384


def draw_waveforms(key, part):
    first_key, second_key, third_key, level_key, wander_key = jax.random.split(key, 5)
    noise_base = jax.random.truncated_normal(first_key, -6.0, 6.0, (CH, NT // 64, 64), jnp.float32)
    envelope = jnp.exp(jax.random.uniform(third_key, (CH, NT // 64, 1), jnp.float32, math.log(0.25), math.log(4.0)))
    level = jax.random.uniform(level_key, (CH, 1, 1), jnp.float32, -2.0, 2.0)
    wander = jax.random.uniform(wander_key, (CH, NT // 1024, 1), jnp.float32, -1.0, 1.0)
    channel_gain = jnp.exp(jax.random.uniform(second_key, (CH, 1, 1), jnp.float32, math.log(0.3), math.log(3.0)))
    offset = level + jnp.repeat(wander, 16, axis=1)
    return ((noise_base * envelope + offset) * channel_gain).reshape(CH, NT).astype(jnp.bfloat16)


def draw_channel_lists(key, part):
    offsets = jax.random.randint(key, (BLOCKS, TPB, TCH), 0, CH_REG, dtype=jnp.int32)
    region_start = jnp.arange(TCH, dtype=jnp.int32) // TCH_REG * CH_REG
    picked = offsets + region_start[None, None, :]
    picked = picked.at[0, 0, 0].set(0)
    picked = picked.at[0, 0, TCH - 1].set(CH - 1)
    return picked.astype(jnp.int32)


def level_of(stream_key, shape, cuts, least, top_value):
    def one(position, shards_of):
        draws = jax.random.uniform(jax.random.fold_in(jax.random.fold_in(stream_key, 6), position), (shards_of,), jnp.float32, least / len(cuts), top_value / len(cuts))
        return jnp.repeat(jnp.exp(draws), shape[position] // shards_of).reshape((-1,) + (1,) * (len(shape) - position - 1))

    gain = one(*cuts[0])
    for cut in cuts[1:]:
        gain = gain * one(*cut)
    return gain


def gaussian(rng, dims, scale, limit, cuts=(), kind=jnp.bfloat16):
    loudness = level_of(rng, dims, cuts, -0.22, 0.18) if cuts else 1.0
    values = jax.random.normal(rng, dims, jnp.float32) * scale * loudness
    return jnp.minimum(jnp.maximum(values, -limit), limit).astype(kind)


def setup_inputs(seed: int = 0) -> dict:
    splits = jax.random.split(jax.random.key(seed), 5)
    return {
        "waveforms": draw_waveforms(jax.random.fold_in(splits[4], 71), 0),
        "templates": gaussian(splits[1], (BLOCKS, TPB, TCH, L), 1.0, 6.0, ((0, 8), (2, 4))),
        "channel_lists": draw_channel_lists(jax.random.fold_in(splits[4], 71), 0),
        "owner_ranks": jax.random.randint(splits[3], (ROUNDS,), 0, BLOCKS).astype(jnp.int32),
    }


def unit_rows(rows_in):
    window_len = rows_in.shape[-1]
    centred = rows_in - lax.optimization_barrier(jnp.mean(rows_in, axis=-1, keepdims=True))
    energy = lax.optimization_barrier(jnp.mean(centred * centred, axis=-1, keepdims=True))
    return (centred / jnp.sqrt(window_len * (energy + 1e-05))).astype(jnp.bfloat16)

def window_sums(series, window_len):
    count = series.shape[0]
    total_blocks = series.shape[1] // 128
    reach = window_len // 128
    out_blocks = total_blocks - reach
    shaped = series.reshape(count, total_blocks, 128)
    running = jnp.cumsum(shaped, axis=2)
    before = jnp.pad(running[:, :, :-1], ((0, 0), (0, 0), (1, 0)))
    block_total = running[:, :, -1]
    result = block_total[:, :out_blocks, None] - before[:, :out_blocks] + before[:, reach:reach + out_blocks]
    for middle in range(1, reach):
        result = result + block_total[:, middle:middle + out_blocks, None]
    return result.reshape(count, out_blocks * 128)

def segments(series, window_len, slab_len):
    count = series.shape[0]
    span_blocks = slab_len // 128
    pieces = [series[:, 128 * step:128 * step + slab_len].reshape(count, span_blocks, 128) for step in range(window_len // 128 + 1)]
    return jnp.concatenate(pieces, axis=2)

def banded(weights):
    count = weights.shape[0]
    span = weights.shape[1] + 128
    padded = jnp.concatenate([weights, jnp.zeros((count, 128), weights.dtype)], axis=1)
    tiled = jnp.tile(padded, (1, 128))[:, :128 * (span - 1)]
    return jnp.pad(tiled.reshape(count, 128, span - 1), ((0, 0), (0, 0), (0, 1)))

def correlate_ref(picked, weights):
    count = picked.shape[0]
    window_len = weights.shape[1]
    slab_len = picked.shape[1] - window_len
    series = picked.astype(jnp.float32)
    pieces = segments(series, window_len, slab_len)
    band_rows = banded(weights.astype(jnp.float32))
    numer = jnp.einsum('rbi,rsi->rbs', pieces, band_rows, precision=lax.Precision.HIGHEST).reshape(count, slab_len)
    first = window_sums(series, window_len)
    second = window_sums(series * series, window_len)
    spread = second / window_len - first / window_len * (first / window_len)
    return numer / jnp.sqrt(window_len * (spread + 1e-05))

def reference(waveforms, templates, channel_lists, owner_ranks):
    window_len = templates.shape[3]
    total_len = waveforms.shape[1]
    pair_ids = jnp.arange(ROUNDS * TPB, dtype=jnp.int32)
    owner_of = owner_ranks[pair_ids // TPB]
    member_of = pair_ids % TPB

    def one_pair(pair):
        owner_id, member_id = pair
        weights = unit_rows(templates[owner_id, member_id].astype(jnp.float32))
        row_ids = channel_lists[owner_id, member_id]
        picked = jnp.pad(waveforms[row_ids], ((0, 0), (0, window_len)))
        scores = correlate_ref(picked, weights)
        return lax.optimization_barrier(jnp.sum(scores, axis=0))
    stacked = lax.map(one_pair, (owner_of, member_of))
    starts = jnp.arange(total_len, dtype=jnp.int32)
    valid_mask = starts <= total_len - window_len
    return jnp.where(valid_mask[None, :], stacked, jnp.float32(0.0))
```

```python
import jax
import jax.numpy as jnp
from jax import lax
from jax.experimental import pallas as pl
from jax.experimental.pallas import tpu as pltpu
from jax.sharding import PartitionSpec as P

LANES = 128
NT_DIMS = (((1,), (1,)), ((), ()))


def unit_rows(rows_in):
    window_len = rows_in.shape[-1]
    centred = rows_in - jnp.mean(rows_in, axis=-1, keepdims=True)
    energy = jnp.mean(centred * centred, axis=-1, keepdims=True)
    return (centred / jnp.sqrt(window_len * (energy + 1e-05))).astype(jnp.bfloat16)


def shifted_rows(rows, upper):
    parts = []
    before = jnp.zeros((LANES, LANES), jnp.bfloat16)
    for at in range(0, rows.shape[1], LANES):
        wide = jnp.broadcast_to(rows[:, at : at + LANES], (LANES, LANES))
        rolled = pltpu.roll(wide, 0, 1, stride=1, stride_axis=0).astype(jnp.bfloat16)
        parts.append(jnp.where(upper, rolled, before))
        before = rolled
    parts.append(jnp.where(upper, jnp.zeros_like(before), before))
    return jnp.concatenate(parts, axis=1)


def kernel(ids_ref, wave_ref, rim_ref, tmpl_ref, out_ref, wide, picked):
    templates, channels, window_len = tmpl_ref.shape
    rows, slab_len = wave_ref.shape
    blocks = slab_len // LANES
    reach = window_len // LANES
    for j in range(blocks):
        wide[j] = wave_ref[:, LANES * j : LANES * (j + 1)].astype(jnp.float32)
    for j in range(reach):
        wide[blocks + j] = rim_ref[:, LANES * j : LANES * (j + 1)].astype(jnp.float32)
    sub = lax.broadcasted_iota(jnp.int32, (LANES, LANES), 0)
    lane = lax.broadcasted_iota(jnp.int32, (LANES, LANES), 1)
    upper = lane >= sub
    ones = jnp.ones((LANES, LANES), jnp.bfloat16)
    zeros = jnp.zeros((LANES, LANES), jnp.bfloat16)
    band = jnp.concatenate(
        [jnp.where(upper, ones, zeros)] + [ones] * (reach - 1) + [jnp.where(upper, zeros, ones)], axis=1
    )

    def one_template(which, carry):
        for c in range(channels):
            row = ids_ref[which, c]
            for j in range(blocks + reach):
                picked[c, j : j + 1, :] = wide[j, pl.ds(row, 1), :]
        units = unit_rows(tmpl_ref[which].astype(jnp.float32)).astype(jnp.float32)
        total = jnp.zeros((blocks, LANES), jnp.float32)
        for c in range(channels):
            pieces = [picked[c, j : j + blocks, :] for j in range(reach + 1)]
            squares = [p * p for p in pieces]
            high = [s.astype(jnp.bfloat16) for s in squares]
            low = [(s - h.astype(jnp.float32)).astype(jnp.bfloat16) for s, h in zip(squares, high)]
            series = jnp.concatenate([p.astype(jnp.bfloat16) for p in pieces], axis=1)
            stacked = jnp.concatenate(
                [series, jnp.concatenate(high, axis=1), jnp.concatenate(low, axis=1)], axis=0
            )
            sums = lax.dot_general(stacked, band, NT_DIMS, preferred_element_type=jnp.float32)
            numer = lax.dot_general(
                series, shifted_rows(units[c : c + 1], upper), NT_DIMS, preferred_element_type=jnp.float32
            )
            mean = sums[:blocks] / window_len
            spread = (sums[blocks : 2 * blocks] + sums[2 * blocks :]) / window_len - mean * mean
            total += numer * lax.rsqrt(window_len * (spread + 1e-05))
        out_ref[which] = total
        return carry

    lax.fori_loop(0, templates, one_template, 0)


def per_device(waveforms, templates, channel_lists, owner_ranks):
    window_len = templates.shape[3]
    channels = templates.shape[2]
    region_rows, slab_len = waveforms.shape
    count = lax.axis_size("tm")
    rank = lax.axis_index("tm")
    rim = lax.ppermute(waveforms[:, :window_len], "tm", [(i, i - 1) for i in range(1, count)])
    mine = (owner_ranks == rank)[:, None, None, None]
    blocks = lax.psum(jnp.where(mine, templates, 0).astype(templates.dtype), "tm")
    tmpl = blocks.reshape(-1, channels, window_len)
    ids = (channel_lists[owner_ranks] - lax.axis_index("region") * region_rows).reshape(-1, channels)
    total = tmpl.shape[0]
    vmem = pl.BlockSpec(memory_space=pltpu.VMEM)
    scores = pl.pallas_call(
        kernel,
        out_shape=jax.ShapeDtypeStruct((total, slab_len // LANES, LANES), jnp.float32),
        in_specs=[pl.BlockSpec(memory_space=pltpu.SMEM), vmem, vmem, vmem],
        out_specs=vmem,
        scratch_shapes=[
            pltpu.VMEM(((slab_len + window_len) // LANES, region_rows, LANES), jnp.float32),
            pltpu.VMEM((channels, (slab_len + window_len) // LANES, LANES), jnp.float32),
        ],
        compiler_params=pltpu.CompilerParams(vmem_limit_bytes=40 << 20),
    )(ids, waveforms, rim, tmpl)
    detection = lax.psum(scores, "region").reshape(total, slab_len)
    total_len = slab_len * count
    starts = rank * slab_len + jnp.arange(slab_len, dtype=jnp.int32)
    return jnp.where((starts <= total_len - window_len)[None, :], detection, jnp.float32(0.0))


def solution(mesh):
    placed = (P("region", "tm"), P("tm", None, "region", None), P(None, None, "region"), P())
    return jax.shard_map(
        per_device, mesh=mesh, in_specs=placed, out_specs=P(None, "tm"), check_vma=False
    )
```

```python
import jax
import jax.numpy as jnp
from jax import lax
from jax.experimental import pallas as pl
from jax.experimental.pallas import tpu as pltpu
from jax.sharding import PartitionSpec as P

LANES = 128
CHUNKS = 4
NT_DIMS = (((1,), (1,)), ((), ()))
MESH = pl.DeviceIdType.MESH


def unit_rows(rows_in):
    window_len = rows_in.shape[-1]
    centred = rows_in - jnp.mean(rows_in, axis=-1, keepdims=True)
    energy = jnp.mean(centred * centred, axis=-1, keepdims=True)
    return (centred / jnp.sqrt(window_len * (energy + 1e-05))).astype(jnp.bfloat16)


def shifted_rows(pieces, upper):
    parts = []
    before = jnp.zeros((LANES, LANES), jnp.bfloat16)
    for piece in pieces:
        wide = jnp.broadcast_to(piece, (LANES, LANES))
        rolled = pltpu.roll(wide, 0, 1, stride=1, stride_axis=0).astype(jnp.bfloat16)
        parts.append(jnp.where(upper, rolled, before))
        before = rolled
    parts.append(jnp.where(upper, jnp.zeros_like(before), before))
    return jnp.concatenate(parts, axis=1)


def kernel(
    count, regions, members, channels,
    owner_ref, lists_ref, wave_ref, tmpl_ref, out_ref,
    wave_v, wide, picked, head, head_out, rim_in, rim, gathered, units, series, inverse, acc, part, res,
    wave_sem, block_send, block_recv, rim_send, rim_recv, part_send, part_recv, res_send, res_recv,
):
    me = lax.axis_index("tm")
    region = lax.axis_index("region")
    rows, slab_len = wave_ref.shape
    window_len = tmpl_ref.shape[1]
    rounds = owner_ref.shape[0]
    padded_rows = tmpl_ref.shape[0]
    total = rounds * members
    blocks = slab_len // LANES
    reach = window_len // LANES
    share = total // regions
    per_chunk = blocks // CHUNKS

    loads = []
    for k in range(CHUNKS):
        cols = slice(k * per_chunk * LANES, (k + 1) * per_chunk * LANES)
        loads.append(pltpu.make_async_copy(wave_ref.at[:, cols], wave_v.at[:, cols], wave_sem.at[k]))
        loads[-1].start()

    barrier = pltpu.get_barrier_semaphore()
    for d in range(1, count):
        pl.semaphore_signal(barrier, inc=1, device_id=(region, lax.rem(me + d, count)), device_id_type=MESH)
    for d in range(1, regions):
        pl.semaphore_signal(barrier, inc=1, device_id=(lax.rem(region + d, regions), me), device_id_type=MESH)
    pl.semaphore_wait(barrier, count + regions - 2)

    sent = []
    for d in range(1, count):
        sent.append(pltpu.make_async_remote_copy(
            src_ref=tmpl_ref, dst_ref=gathered.at[me], send_sem=block_send.at[d], recv_sem=block_recv.at[d],
            device_id=(region, lax.rem(me + d, count)), device_id_type=MESH))
        sent[-1].start()
    gathered[me] = tmpl_ref[...]

    base = region * rows

    def pick(first, last):
        def body(which, carry):
            owner = owner_ref[which // members]
            for c in range(channels):
                row = jnp.clip(lists_ref[owner, lax.rem(which, members), c] - base, 0, rows - 1)
                at = which * channels + c
                for j in range(first, last):
                    value = wide[j, pl.ds(row, 1), :]
                    picked[at, j : j + 1, :] = value
                    if j < reach:
                        head[j, pl.ds(at, 1), :] = value
            return carry

        lax.fori_loop(0, total, body, 0)

    rim_copy = pltpu.make_async_remote_copy(
        src_ref=head_out, dst_ref=rim_in, send_sem=rim_send, recv_sem=rim_recv,
        device_id=(region, lax.rem(me + count - 1, count)), device_id_type=MESH)
    for k in range(CHUNKS):
        loads[k].wait()
        for j in range(k * per_chunk, (k + 1) * per_chunk):
            wide[j] = wave_v[:, LANES * j : LANES * (j + 1)].astype(jnp.float32)
        pick(k * per_chunk, (k + 1) * per_chunk)
        if k == 0:
            head_out[...] = head[...].astype(jnp.bfloat16)
            rim_copy.start()

    sub = lax.broadcasted_iota(jnp.int32, (LANES, LANES), 0)
    lane = lax.broadcasted_iota(jnp.int32, (LANES, LANES), 1)
    upper = lane >= sub
    ones = jnp.ones((LANES, LANES), jnp.bfloat16)
    zeros = jnp.zeros((LANES, LANES), jnp.bfloat16)
    band = jnp.concatenate(
        [jnp.where(upper, ones, zeros)] + [ones] * (reach - 1) + [jnp.where(upper, zeros, ones)], axis=1
    )

    rim_copy.wait()
    inner = (me < count - 1).astype(jnp.float32)
    rim[...] = rim_in[...].astype(jnp.float32) * inner

    def window_sums(which, carry):
        stacked = []
        for c in range(channels):
            at = which * channels + c
            for j in range(reach):
                picked[at, blocks + j : blocks + j + 1, :] = rim[j, pl.ds(at, 1), :]
            pieces = [picked[at, j : j + blocks, :] for j in range(reach + 1)]
            squares = [p * p for p in pieces]
            high = [s.astype(jnp.bfloat16) for s in squares]
            low = [(s - h.astype(jnp.float32)).astype(jnp.bfloat16) for s, h in zip(squares, high)]
            record = jnp.concatenate([p.astype(jnp.bfloat16) for p in pieces], axis=1)
            series[at] = record
            stacked += [record, jnp.concatenate(high, axis=1), jnp.concatenate(low, axis=1)]
        sums = lax.dot_general(
            jnp.concatenate(stacked, axis=0), band, NT_DIMS, preferred_element_type=jnp.float32
        ).reshape(channels, 3, blocks, LANES)
        mean = sums[:, 0] / window_len
        spread = (sums[:, 1] + sums[:, 2]) / window_len - mean * mean
        inverse[pl.ds(which * channels, channels)] = lax.rsqrt(window_len * (spread + 1e-05))
        return carry

    lax.fori_loop(0, total, window_sums, 0)

    for d in range(1, count):
        source = lax.rem(me + count - d, count)
        pltpu.make_async_remote_copy(
            src_ref=tmpl_ref, dst_ref=gathered.at[source], send_sem=block_send.at[d], recv_sem=block_recv.at[d],
            device_id=(region, source), device_id_type=MESH).wait_recv()
    for r in range(rounds):
        unit = unit_rows(gathered[owner_ref[r]].astype(jnp.float32)).astype(jnp.float32)
        for j in range(reach):
            units[j, r * padded_rows : (r + 1) * padded_rows, :] = unit[:, LANES * j : LANES * (j + 1)]

    def scores(which):
        total_value = jnp.zeros((blocks, LANES), jnp.float32)
        first = which // members * padded_rows + lax.rem(which, members) * channels
        for c in range(channels):
            pieces = [units[j, pl.ds(first + c, 1), :] for j in range(reach)]
            numer = lax.dot_general(
                series[which * channels + c], shifted_rows(pieces, upper), NT_DIMS,
                preferred_element_type=jnp.float32)
            total_value += numer * inverse[which * channels + c]
        acc[which] = total_value

    parts = []
    for k in range(regions):
        quarter = lax.rem(region + 1 + k, regions)

        def body(i, carry):
            scores(quarter * share + i)
            return carry

        lax.fori_loop(0, share, body, 0)
        if k < regions - 1:
            parts.append(pltpu.make_async_remote_copy(
                src_ref=acc.at[pl.ds(quarter * share, share)], dst_ref=part.at[k],
                send_sem=part_send.at[k], recv_sem=part_recv.at[k],
                device_id=(quarter, me), device_id_type=MESH))
            parts[-1].start()

    own = pl.ds(region * share, share)
    value = acc[own]
    for k in range(regions - 1):
        parts[k].wait_recv()
        value += part[k]
    res[own] = value
    results = []
    for d in range(1, regions):
        results.append(pltpu.make_async_remote_copy(
            src_ref=res.at[own], dst_ref=res.at[own], send_sem=res_send.at[d], recv_sem=res_recv.at[d],
            device_id=(lax.rem(region + d, regions), me), device_id_type=MESH))
        results[-1].start()
    for d in range(1, regions):
        source = lax.rem(region + regions - d, regions)
        theirs = pl.ds(source * share, share)
        pltpu.make_async_remote_copy(
            src_ref=res.at[theirs], dst_ref=res.at[theirs], send_sem=res_send.at[d], recv_sem=res_recv.at[d],
            device_id=(source, me), device_id_type=MESH).wait_recv()
    for j in range(blocks):
        out_ref[:, LANES * j : LANES * (j + 1)] = res[:, j, :]
    for copy in sent + parts + results:
        copy.wait_send()


def per_device(waveforms, templates, channel_lists, owner_ranks):
    members, channels, window_len = templates.shape[1:]
    region_rows, slab_len = waveforms.shape
    count = lax.axis_size("tm")
    regions = lax.axis_size("region")
    rounds = owner_ranks.shape[0]
    total = rounds * members
    pairs = total * channels
    blocks = slab_len // LANES
    reach = window_len // LANES
    padded_rows = -(-members * channels // 16) * 16
    flat = templates.reshape(members * channels, window_len)
    flat = jnp.pad(flat, ((0, padded_rows - members * channels), (0, 0)))
    share = total // regions
    vmem = pl.BlockSpec(memory_space=pltpu.VMEM)
    smem = pl.BlockSpec(memory_space=pltpu.SMEM)
    dma = pltpu.SemaphoreType.DMA

    def body(*refs):
        kernel(count, regions, members, channels, *refs)

    detection = pl.pallas_call(
        body,
        out_shape=jax.ShapeDtypeStruct((total, slab_len), jnp.float32),
        in_specs=[smem, smem, pl.BlockSpec(memory_space=pl.ANY), vmem],
        out_specs=vmem,
        scratch_shapes=[
            pltpu.VMEM((region_rows, slab_len), jnp.bfloat16),
            pltpu.VMEM((blocks, region_rows, LANES), jnp.float32),
            pltpu.VMEM((pairs, blocks + reach, LANES), jnp.float32),
            pltpu.VMEM((reach, pairs, LANES), jnp.float32),
            pltpu.VMEM((reach, pairs, LANES), jnp.bfloat16),
            pltpu.VMEM((reach, pairs, LANES), jnp.bfloat16),
            pltpu.VMEM((reach, pairs, LANES), jnp.float32),
            pltpu.VMEM((count, padded_rows, window_len), jnp.bfloat16),
            pltpu.VMEM((reach, rounds * padded_rows, LANES), jnp.float32),
            pltpu.VMEM((pairs, blocks, LANES + window_len), jnp.bfloat16),
            pltpu.VMEM((pairs, blocks, LANES), jnp.float32),
            pltpu.VMEM((total, blocks, LANES), jnp.float32),
            pltpu.VMEM((regions - 1, share, blocks, LANES), jnp.float32),
            pltpu.VMEM((total, blocks, LANES), jnp.float32),
            dma((CHUNKS,)),
            dma((count,)),
            dma((count,)),
            dma,
            dma,
            dma((regions,)),
            dma((regions,)),
            dma((regions,)),
            dma((regions,)),
        ],
        compiler_params=pltpu.CompilerParams(
            vmem_limit_bytes=48 << 20, collective_id=0, has_side_effects=True
        ),
    )(owner_ranks, channel_lists, waveforms, flat)
    starts = lax.axis_index("tm") * slab_len + jnp.arange(slab_len, dtype=jnp.int32)
    return jnp.where((starts <= slab_len * count - window_len)[None, :], detection, jnp.float32(0.0))


def solution(mesh):
    placed = (P("region", "tm"), P("tm", None, "region", None), P(None, None, "region"), P())
    return jax.shard_map(
        per_device, mesh=mesh, in_specs=placed, out_specs=P(None, "tm"), check_vma=False
    )
```

```python
import jax
import jax.numpy as jnp
from jax import lax
from jax.experimental import pallas as pl
from jax.experimental.pallas import tpu as pltpu
from jax.sharding import PartitionSpec as P

LANES = 128
CHUNKS = 4
EARLY = 2
NT_DIMS = (((1,), (1,)), ((), ()))
MESH = pl.DeviceIdType.MESH


def unit_rows(rows_in):
    window_len = rows_in.shape[-1]
    centred = rows_in - jnp.mean(rows_in, axis=-1, keepdims=True)
    energy = jnp.mean(centred * centred, axis=-1, keepdims=True)
    return (centred / jnp.sqrt(window_len * (energy + 1e-05))).astype(jnp.bfloat16)


def shifted_rows(pieces, upper):
    parts = []
    before = jnp.zeros((LANES, LANES), jnp.bfloat16)
    for piece in pieces:
        wide = jnp.broadcast_to(piece, (LANES, LANES))
        rolled = pltpu.roll(wide, 0, 1, stride=1, stride_axis=0).astype(jnp.bfloat16)
        parts.append(jnp.where(upper, rolled, before))
        before = rolled
    parts.append(jnp.where(upper, jnp.zeros_like(before), before))
    return jnp.concatenate(parts, axis=1)


def kernel(
    count, regions, members, channels,
    owner_hbm, lists_hbm, wave_ref, tmpl_hbm, out_ref,
    owner_ref, lists_ref, tmpl_v, flat, small_sem, wave_v, wide, picked, head, head_out, rim_in, rim, gathered, units, series, inverse, acc, part, res,
    wave_sem, block_send, block_recv, rim_send, rim_recv, part_send, part_recv, res_send, res_recv,
):
    me = lax.axis_index("tm")
    region = lax.axis_index("region")
    rows, slab_len = wave_ref.shape
    window_len = tmpl_v.shape[2]
    rounds = owner_ref.shape[0]
    padded_rows = flat.shape[0]
    total = rounds * members
    blocks = slab_len // LANES
    reach = window_len // LANES
    share = total // regions
    per_chunk = blocks // CHUNKS

    barrier = pltpu.get_barrier_semaphore()
    for d in range(1, count):
        pl.semaphore_signal(barrier, inc=1, device_id=(region, lax.rem(me + d, count)), device_id_type=MESH)
    for d in range(1, regions):
        pl.semaphore_signal(barrier, inc=1, device_id=(lax.rem(region + d, regions), me), device_id_type=MESH)

    small = [
        pltpu.make_async_copy(owner_hbm, owner_ref, small_sem.at[0]),
        pltpu.make_async_copy(lists_hbm, lists_ref, small_sem.at[1]),
        pltpu.make_async_copy(tmpl_hbm.at[0], tmpl_v, small_sem.at[2]),
    ]
    for copy in small:
        copy.start()
    loads = []
    for k in range(CHUNKS):
        cols = slice(k * per_chunk * LANES, (k + 1) * per_chunk * LANES)
        loads.append(pltpu.make_async_copy(wave_ref.at[:, cols], wave_v.at[:, cols], wave_sem.at[k]))
        loads[-1].start()
    for copy in small:
        copy.wait()
    for t in range(members):
        flat[t * channels : (t + 1) * channels, :] = tmpl_v[t].astype(jnp.float32)
    if padded_rows > members * channels:
        flat[members * channels :, :] = jnp.zeros((padded_rows - members * channels, window_len), jnp.float32)
    gathered[me] = flat[...].astype(jnp.bfloat16)

    base = region * rows

    def pick(first, last):
        def body(which, carry):
            owner = owner_ref[which // members]
            for c in range(channels):
                row = jnp.clip(lists_ref[owner, lax.rem(which, members), c] - base, 0, rows - 1)
                at = which * channels + c
                for j in range(first, last):
                    value = wide[j, pl.ds(row, 1), :]
                    picked[at, j : j + 1, :] = value
                    if j < reach:
                        head[j, pl.ds(at, 1), :] = value
            return carry

        lax.fori_loop(0, total, body, 0)

    rim_copy = pltpu.make_async_remote_copy(
        src_ref=head_out, dst_ref=rim_in, send_sem=rim_send, recv_sem=rim_recv,
        device_id=(region, lax.rem(me + count - 1, count)), device_id_type=MESH)
    sent = []
    for k in range(CHUNKS):
        loads[k].wait()
        for j in range(k * per_chunk, (k + 1) * per_chunk):
            wide[j] = wave_v[:, LANES * j : LANES * (j + 1)].astype(jnp.float32)
        pick(k * per_chunk, (k + 1) * per_chunk)
        if k == EARLY - 1:
            head_out[...] = head[...].astype(jnp.bfloat16)
            pl.semaphore_wait(barrier, count + regions - 2)
            rim_copy.start()
            for d in range(1, count):
                sent.append(pltpu.make_async_remote_copy(
                    src_ref=gathered.at[me], dst_ref=gathered.at[me],
                    send_sem=block_send.at[d], recv_sem=block_recv.at[d],
                    device_id=(region, lax.rem(me + d, count)), device_id_type=MESH))
                sent[-1].start()

    sub = lax.broadcasted_iota(jnp.int32, (LANES, LANES), 0)
    lane = lax.broadcasted_iota(jnp.int32, (LANES, LANES), 1)
    upper = lane >= sub
    ones = jnp.ones((LANES, LANES), jnp.bfloat16)
    zeros = jnp.zeros((LANES, LANES), jnp.bfloat16)
    band = jnp.concatenate(
        [jnp.where(upper, ones, zeros)] + [ones] * (reach - 1) + [jnp.where(upper, zeros, ones)], axis=1
    )

    rim_copy.wait()
    inner = (me < count - 1).astype(jnp.float32)
    rim[...] = rim_in[...].astype(jnp.float32) * inner

    def window_sums(which, carry):
        stacked = []
        for c in range(channels):
            at = which * channels + c
            for j in range(reach):
                picked[at, blocks + j : blocks + j + 1, :] = rim[j, pl.ds(at, 1), :]
            pieces = [picked[at, j : j + blocks, :] for j in range(reach + 1)]
            squares = [p * p for p in pieces]
            high = [s.astype(jnp.bfloat16) for s in squares]
            low = [(s - h.astype(jnp.float32)).astype(jnp.bfloat16) for s, h in zip(squares, high)]
            record = jnp.concatenate([p.astype(jnp.bfloat16) for p in pieces], axis=1)
            series[at] = record
            stacked += [record, jnp.concatenate(high, axis=1), jnp.concatenate(low, axis=1)]
        sums = lax.dot_general(
            jnp.concatenate(stacked, axis=0), band, NT_DIMS, preferred_element_type=jnp.float32
        ).reshape(channels, 3, blocks, LANES)
        mean = sums[:, 0] / window_len
        spread = (sums[:, 1] + sums[:, 2]) / window_len - mean * mean
        inverse[pl.ds(which * channels, channels)] = lax.rsqrt(window_len * (spread + 1e-05))
        return carry

    lax.fori_loop(0, total, window_sums, 0)

    for d in range(1, count):
        source = lax.rem(me + count - d, count)
        pltpu.make_async_remote_copy(
            src_ref=gathered.at[source], dst_ref=gathered.at[source], send_sem=block_send.at[d], recv_sem=block_recv.at[d],
            device_id=(region, source), device_id_type=MESH).wait_recv()
    for r in range(rounds):
        unit = unit_rows(gathered[owner_ref[r]].astype(jnp.float32)).astype(jnp.float32)
        for j in range(reach):
            units[j, r * padded_rows : (r + 1) * padded_rows, :] = unit[:, LANES * j : LANES * (j + 1)]

    def scores(which):
        total_value = jnp.zeros((blocks, LANES), jnp.float32)
        first = which // members * padded_rows + lax.rem(which, members) * channels
        for c in range(channels):
            pieces = [units[j, pl.ds(first + c, 1), :] for j in range(reach)]
            numer = lax.dot_general(
                series[which * channels + c], shifted_rows(pieces, upper), NT_DIMS,
                preferred_element_type=jnp.float32)
            total_value += numer * inverse[which * channels + c]
        acc[which] = total_value

    parts = []
    for k in range(regions):
        quarter = lax.rem(region + 1 + k, regions)

        def body(i, carry):
            scores(quarter * share + i)
            return carry

        lax.fori_loop(0, share, body, 0)
        if k < regions - 1:
            parts.append(pltpu.make_async_remote_copy(
                src_ref=acc.at[pl.ds(quarter * share, share)], dst_ref=part.at[k],
                send_sem=part_send.at[k], recv_sem=part_recv.at[k],
                device_id=(quarter, me), device_id_type=MESH))
            parts[-1].start()

    own = pl.ds(region * share, share)
    value = acc[own]
    for k in range(regions - 1):
        parts[k].wait_recv()
        value += part[k]
    res[own] = value
    results = []
    for d in range(1, regions):
        results.append(pltpu.make_async_remote_copy(
            src_ref=res.at[own], dst_ref=res.at[own], send_sem=res_send.at[d], recv_sem=res_recv.at[d],
            device_id=(lax.rem(region + d, regions), me), device_id_type=MESH))
        results[-1].start()
    for d in range(1, regions):
        source = lax.rem(region + regions - d, regions)
        theirs = pl.ds(source * share, share)
        pltpu.make_async_remote_copy(
            src_ref=res.at[theirs], dst_ref=res.at[theirs], send_sem=res_send.at[d], recv_sem=res_recv.at[d],
            device_id=(source, me), device_id_type=MESH).wait_recv()
    for j in range(blocks):
        out_ref[:, LANES * j : LANES * (j + 1)] = res[:, j, :]
    for copy in sent + parts + results:
        copy.wait_send()


def per_device(waveforms, templates, channel_lists, owner_ranks):
    members, channels, window_len = templates.shape[1:]
    region_rows, slab_len = waveforms.shape
    count = lax.axis_size("tm")
    regions = lax.axis_size("region")
    rounds = owner_ranks.shape[0]
    total = rounds * members
    pairs = total * channels
    blocks = slab_len // LANES
    reach = window_len // LANES
    padded_rows = -(-members * channels // 16) * 16
    share = total // regions
    vmem = pl.BlockSpec(memory_space=pltpu.VMEM)
    hbm = pl.BlockSpec(memory_space=pl.ANY)
    dma = pltpu.SemaphoreType.DMA

    def body(*refs):
        kernel(count, regions, members, channels, *refs)

    detection = pl.pallas_call(
        body,
        out_shape=jax.ShapeDtypeStruct((total, slab_len), jnp.float32),
        in_specs=[hbm] * 4,
        out_specs=vmem,
        scratch_shapes=[
            pltpu.SMEM(owner_ranks.shape, jnp.int32),
            pltpu.SMEM(channel_lists.shape, jnp.int32),
            pltpu.VMEM((members, channels, window_len), jnp.bfloat16),
            pltpu.VMEM((padded_rows, window_len), jnp.float32),
            dma((3,)),
            pltpu.VMEM((region_rows, slab_len), jnp.bfloat16),
            pltpu.VMEM((blocks, region_rows, LANES), jnp.float32),
            pltpu.VMEM((pairs, blocks + reach, LANES), jnp.float32),
            pltpu.VMEM((reach, pairs, LANES), jnp.float32),
            pltpu.VMEM((reach, pairs, LANES), jnp.bfloat16),
            pltpu.VMEM((reach, pairs, LANES), jnp.bfloat16),
            pltpu.VMEM((reach, pairs, LANES), jnp.float32),
            pltpu.VMEM((count, padded_rows, window_len), jnp.bfloat16),
            pltpu.VMEM((reach, rounds * padded_rows, LANES), jnp.float32),
            pltpu.VMEM((pairs, blocks, LANES + window_len), jnp.bfloat16),
            pltpu.VMEM((pairs, blocks, LANES), jnp.float32),
            pltpu.VMEM((total, blocks, LANES), jnp.float32),
            pltpu.VMEM((regions - 1, share, blocks, LANES), jnp.float32),
            pltpu.VMEM((total, blocks, LANES), jnp.float32),
            dma((CHUNKS,)),
            dma((count,)),
            dma((count,)),
            dma,
            dma,
            dma((regions,)),
            dma((regions,)),
            dma((regions,)),
            dma((regions,)),
        ],
        compiler_params=pltpu.CompilerParams(
            vmem_limit_bytes=60 << 20, collective_id=0, has_side_effects=True
        ),
    )(owner_ranks, channel_lists, waveforms, templates)
    starts = lax.axis_index("tm") * slab_len + jnp.arange(slab_len, dtype=jnp.int32)
    return jnp.where((starts <= slab_len * count - window_len)[None, :], detection, jnp.float32(0.0))


def solution(mesh):
    placed = (P("region", "tm"), P("tm", None, "region", None), P(None, None, "region"), P())
    return jax.shard_map(
        per_device, mesh=mesh, in_specs=placed, out_specs=P(None, "tm"), check_vma=False
    )
```

```python
import jax
import jax.numpy as jnp
from jax import lax
from jax.experimental import pallas as pl
from jax.experimental.pallas import tpu as pltpu
from jax.sharding import PartitionSpec as P

LANES = 128
CHUNKS = 4
EARLY = 2
NT_DIMS = (((1,), (1,)), ((), ()))
MESH = pl.DeviceIdType.MESH


def unit_rows(rows_in):
    window_len = rows_in.shape[-1]
    centred = rows_in - jnp.mean(rows_in, axis=-1, keepdims=True)
    energy = jnp.mean(centred * centred, axis=-1, keepdims=True)
    return (centred / jnp.sqrt(window_len * (energy + 1e-05))).astype(jnp.bfloat16)


def shifted_rows(pieces, upper):
    parts = []
    before = jnp.zeros((LANES, LANES), jnp.bfloat16)
    for piece in pieces:
        wide = jnp.broadcast_to(piece, (LANES, LANES))
        rolled = pltpu.roll(wide, 0, 1, stride=1, stride_axis=0).astype(jnp.bfloat16)
        parts.append(jnp.where(upper, rolled, before))
        before = rolled
    parts.append(jnp.where(upper, jnp.zeros_like(before), before))
    return jnp.concatenate(parts, axis=1)


def kernel(
    count, regions, members, channels,
    owner_hbm, lists_hbm, wave_ref, tmpl_hbm, out_ref,
    owner_ref, lists_ref, tmpl_v, flat, small_sem, wave_v, wide, picked, head, head_out, rim_in, rim, gathered, units, series, inverse, acc, part, res,
    wave_sem, block_send, block_recv, rim_send, rim_recv, part_send, part_recv, res_send, res_recv,
):
    me = lax.axis_index("tm")
    region = lax.axis_index("region")
    rows, slab_len = wave_ref.shape
    window_len = tmpl_v.shape[2]
    rounds = owner_ref.shape[0]
    padded_rows = flat.shape[0]
    total = rounds * members
    blocks = slab_len // LANES
    reach = window_len // LANES
    share = total // regions
    per_chunk = blocks // CHUNKS

    barrier = pltpu.get_barrier_semaphore()
    for d in range(1, count):
        pl.semaphore_signal(barrier, inc=1, device_id=(region, lax.rem(me + d, count)), device_id_type=MESH)
    for d in range(1, regions):
        pl.semaphore_signal(barrier, inc=1, device_id=(lax.rem(region + d, regions), me), device_id_type=MESH)

    small = [
        pltpu.make_async_copy(owner_hbm, owner_ref, small_sem.at[0]),
        pltpu.make_async_copy(lists_hbm, lists_ref, small_sem.at[1]),
        pltpu.make_async_copy(tmpl_hbm, tmpl_v, small_sem.at[2]),
    ]
    for copy in small:
        copy.start()
    loads = []
    for k in range(CHUNKS):
        cols = slice(k * per_chunk * LANES, (k + 1) * per_chunk * LANES)
        loads.append(pltpu.make_async_copy(wave_ref.at[:, cols], wave_v.at[:, cols], wave_sem.at[k]))
        loads[-1].start()
    for copy in small:
        copy.wait()
    for c in range(channels):
        flat[c * members : (c + 1) * members, :] = tmpl_v[c].astype(jnp.float32)
    if padded_rows > members * channels:
        flat[members * channels :, :] = jnp.zeros((padded_rows - members * channels, window_len), jnp.float32)
    gathered[me] = flat[...].astype(jnp.bfloat16)

    base = region * rows

    def pick(first, last):
        def body(which, carry):
            owner = owner_ref[which // members]
            for c in range(channels):
                row = jnp.clip(lists_ref[owner, lax.rem(which, members), c] - base, 0, rows - 1)
                at = which * channels + c
                for j in range(first, last):
                    value = wide[j, pl.ds(row, 1), :]
                    picked[at, j : j + 1, :] = value
                    if j < reach:
                        head[j, pl.ds(at, 1), :] = value
            return carry

        lax.fori_loop(0, total, body, 0)

    rim_copy = pltpu.make_async_remote_copy(
        src_ref=head_out, dst_ref=rim_in, send_sem=rim_send, recv_sem=rim_recv,
        device_id=(region, lax.rem(me + count - 1, count)), device_id_type=MESH)
    sent = []
    for k in range(CHUNKS):
        loads[k].wait()
        for j in range(k * per_chunk, (k + 1) * per_chunk):
            wide[j] = wave_v[:, LANES * j : LANES * (j + 1)].astype(jnp.float32)
        pick(k * per_chunk, (k + 1) * per_chunk)
        if k == EARLY - 1:
            head_out[...] = head[...].astype(jnp.bfloat16)
            pl.semaphore_wait(barrier, count + regions - 2)
            rim_copy.start()
            for d in range(1, count):
                sent.append(pltpu.make_async_remote_copy(
                    src_ref=gathered.at[me], dst_ref=gathered.at[me],
                    send_sem=block_send.at[d], recv_sem=block_recv.at[d],
                    device_id=(region, lax.rem(me + d, count)), device_id_type=MESH))
                sent[-1].start()

    sub = lax.broadcasted_iota(jnp.int32, (LANES, LANES), 0)
    lane = lax.broadcasted_iota(jnp.int32, (LANES, LANES), 1)
    upper = lane >= sub
    ones = jnp.ones((LANES, LANES), jnp.bfloat16)
    zeros = jnp.zeros((LANES, LANES), jnp.bfloat16)
    band = jnp.concatenate(
        [jnp.where(upper, ones, zeros)] + [ones] * (reach - 1) + [jnp.where(upper, zeros, ones)], axis=1
    )

    rim_copy.wait()
    inner = (me < count - 1).astype(jnp.float32)
    rim[...] = rim_in[...].astype(jnp.float32) * inner

    def window_sums(which, carry):
        stacked = []
        for c in range(channels):
            at = which * channels + c
            for j in range(reach):
                picked[at, blocks + j : blocks + j + 1, :] = rim[j, pl.ds(at, 1), :]
            pieces = [picked[at, j : j + blocks, :] for j in range(reach + 1)]
            squares = [p * p for p in pieces]
            high = [s.astype(jnp.bfloat16) for s in squares]
            low = [(s - h.astype(jnp.float32)).astype(jnp.bfloat16) for s, h in zip(squares, high)]
            record = jnp.concatenate([p.astype(jnp.bfloat16) for p in pieces], axis=1)
            series[at] = record
            stacked += [record, jnp.concatenate(high, axis=1), jnp.concatenate(low, axis=1)]
        sums = lax.dot_general(
            jnp.concatenate(stacked, axis=0), band, NT_DIMS, preferred_element_type=jnp.float32
        ).reshape(channels, 3, blocks, LANES)
        mean = sums[:, 0] / window_len
        spread = (sums[:, 1] + sums[:, 2]) / window_len - mean * mean
        inverse[pl.ds(which * channels, channels)] = lax.rsqrt(window_len * (spread + 1e-05))
        return carry

    lax.fori_loop(0, total, window_sums, 0)

    for d in range(1, count):
        source = lax.rem(me + count - d, count)
        pltpu.make_async_remote_copy(
            src_ref=gathered.at[source], dst_ref=gathered.at[source], send_sem=block_send.at[d], recv_sem=block_recv.at[d],
            device_id=(region, source), device_id_type=MESH).wait_recv()
    for r in range(rounds):
        unit = unit_rows(gathered[owner_ref[r]].astype(jnp.float32)).astype(jnp.float32)
        for j in range(reach):
            units[j, r * padded_rows : (r + 1) * padded_rows, :] = unit[:, LANES * j : LANES * (j + 1)]

    def scores(which):
        total_value = jnp.zeros((blocks, LANES), jnp.float32)
        first = which // members * padded_rows + lax.rem(which, members)
        for c in range(channels):
            pieces = [units[j, pl.ds(first + c * members, 1), :] for j in range(reach)]
            numer = lax.dot_general(
                series[which * channels + c], shifted_rows(pieces, upper), NT_DIMS,
                preferred_element_type=jnp.float32)
            total_value += numer * inverse[which * channels + c]
        acc[which] = total_value

    parts = []
    for k in range(regions):
        quarter = lax.rem(region + 1 + k, regions)

        def body(i, carry):
            scores(quarter * share + i)
            return carry

        lax.fori_loop(0, share, body, 0)
        if k < regions - 1:
            parts.append(pltpu.make_async_remote_copy(
                src_ref=acc.at[pl.ds(quarter * share, share)], dst_ref=part.at[k],
                send_sem=part_send.at[k], recv_sem=part_recv.at[k],
                device_id=(quarter, me), device_id_type=MESH))
            parts[-1].start()

    own = pl.ds(region * share, share)
    value = acc[own]
    for k in range(regions - 1):
        parts[k].wait_recv()
        value += part[k]
    res[own] = value
    results = []
    for d in range(1, regions):
        results.append(pltpu.make_async_remote_copy(
            src_ref=res.at[own], dst_ref=res.at[own], send_sem=res_send.at[d], recv_sem=res_recv.at[d],
            device_id=(lax.rem(region + d, regions), me), device_id_type=MESH))
        results[-1].start()
    for d in range(1, regions):
        source = lax.rem(region + regions - d, regions)
        theirs = pl.ds(source * share, share)
        pltpu.make_async_remote_copy(
            src_ref=res.at[theirs], dst_ref=res.at[theirs], send_sem=res_send.at[d], recv_sem=res_recv.at[d],
            device_id=(source, me), device_id_type=MESH).wait_recv()
    for j in range(blocks):
        out_ref[:, LANES * j : LANES * (j + 1)] = res[:, j, :]
    for copy in sent + parts + results:
        copy.wait_send()


def per_device(waveforms, templates, channel_lists, owner_ranks):
    members, channels, window_len = templates.shape[1:]
    region_rows, slab_len = waveforms.shape
    count = lax.axis_size("tm")
    regions = lax.axis_size("region")
    rounds = owner_ranks.shape[0]
    total = rounds * members
    pairs = total * channels
    blocks = slab_len // LANES
    reach = window_len // LANES
    padded_rows = -(-members * channels // 16) * 16
    share = total // regions
    vmem = pl.BlockSpec(memory_space=pltpu.VMEM)
    hbm = pl.BlockSpec(memory_space=pl.ANY)
    dma = pltpu.SemaphoreType.DMA

    def body(*refs):
        kernel(count, regions, members, channels, *refs)

    detection = pl.pallas_call(
        body,
        out_shape=jax.ShapeDtypeStruct((total, slab_len), jnp.float32),
        in_specs=[hbm] * 4,
        out_specs=vmem,
        scratch_shapes=[
            pltpu.SMEM(owner_ranks.shape, jnp.int32),
            pltpu.SMEM(channel_lists.shape, jnp.int32),
            pltpu.VMEM((channels, members, window_len), jnp.bfloat16),
            pltpu.VMEM((padded_rows, window_len), jnp.float32),
            dma((3,)),
            pltpu.VMEM((region_rows, slab_len), jnp.bfloat16),
            pltpu.VMEM((blocks, region_rows, LANES), jnp.float32),
            pltpu.VMEM((pairs, blocks + reach, LANES), jnp.float32),
            pltpu.VMEM((reach, pairs, LANES), jnp.float32),
            pltpu.VMEM((reach, pairs, LANES), jnp.bfloat16),
            pltpu.VMEM((reach, pairs, LANES), jnp.bfloat16),
            pltpu.VMEM((reach, pairs, LANES), jnp.float32),
            pltpu.VMEM((count, padded_rows, window_len), jnp.bfloat16),
            pltpu.VMEM((reach, rounds * padded_rows, LANES), jnp.float32),
            pltpu.VMEM((pairs, blocks, LANES + window_len), jnp.bfloat16),
            pltpu.VMEM((pairs, blocks, LANES), jnp.float32),
            pltpu.VMEM((total, blocks, LANES), jnp.float32),
            pltpu.VMEM((regions - 1, share, blocks, LANES), jnp.float32),
            pltpu.VMEM((total, blocks, LANES), jnp.float32),
            dma((CHUNKS,)),
            dma((count,)),
            dma((count,)),
            dma,
            dma,
            dma((regions,)),
            dma((regions,)),
            dma((regions,)),
            dma((regions,)),
        ],
        compiler_params=pltpu.CompilerParams(
            vmem_limit_bytes=56 << 20, collective_id=0, has_side_effects=True
        ),
    )(owner_ranks, channel_lists, waveforms, templates[0].transpose(1, 0, 2))
    starts = lax.axis_index("tm") * slab_len + jnp.arange(slab_len, dtype=jnp.int32)
    return jnp.where((starts <= slab_len * count - window_len)[None, :], detection, jnp.float32(0.0))


def solution(mesh):
    placed = (P("region", "tm"), P("tm", None, "region", None), P(None, None, "region"), P())
    return jax.shard_map(
        per_device, mesh=mesh, in_specs=placed, out_specs=P(None, "tm"), check_vma=False
    )
```

```python
import jax
import jax.numpy as jnp
from jax import lax
from jax.experimental import pallas as pl
from jax.experimental.pallas import tpu as pltpu
from jax.sharding import PartitionSpec as P

LANES = 128
CHUNKS = 4
EARLY = 2
NT_DIMS = (((1,), (1,)), ((), ()))
MESH = pl.DeviceIdType.MESH


def unit_rows(rows_in):
    window_len = rows_in.shape[-1]
    centred = rows_in - jnp.mean(rows_in, axis=-1, keepdims=True)
    energy = jnp.mean(centred * centred, axis=-1, keepdims=True)
    return (centred / jnp.sqrt(window_len * (energy + 1e-05))).astype(jnp.bfloat16)


def shifted_rows(pieces, upper):
    parts = []
    before = jnp.zeros((LANES, LANES), jnp.bfloat16)
    for piece in pieces:
        wide = jnp.broadcast_to(piece, (LANES, LANES))
        rolled = pltpu.roll(wide, 0, 1, stride=1, stride_axis=0).astype(jnp.bfloat16)
        parts.append(jnp.where(upper, rolled, before))
        before = rolled
    parts.append(jnp.where(upper, jnp.zeros_like(before), before))
    return jnp.concatenate(parts, axis=1)


def kernel(
    count, regions, members, channels,
    owner_hbm, lists_hbm, wave_ref, tmpl_hbm, out_ref,
    owner_ref, lists_ref, tmpl_v, flat, small_sem, wave_v, wide, picked, head, head_out, rim_in, rim, gathered, units, series, inverse, acc, part, res,
    wave_sem, block_send, block_recv, rim_send, rim_recv, part_send, part_recv, res_send, res_recv,
):
    me = lax.axis_index("tm")
    region = lax.axis_index("region")
    rows, slab_len = wave_ref.shape
    window_len = tmpl_v.shape[2]
    rounds = owner_ref.shape[0]
    padded_rows = flat.shape[0]
    total = rounds * members
    blocks = slab_len // LANES
    reach = window_len // LANES
    share = total // regions
    per_chunk = blocks // CHUNKS

    barrier = pltpu.get_barrier_semaphore()
    for d in range(1, count):
        pl.semaphore_signal(barrier, inc=1, device_id=(region, lax.rem(me + d, count)), device_id_type=MESH)
    for d in range(1, regions):
        pl.semaphore_signal(barrier, inc=1, device_id=(lax.rem(region + d, regions), me), device_id_type=MESH)

    small = [
        pltpu.make_async_copy(owner_hbm, owner_ref, small_sem.at[0]),
        pltpu.make_async_copy(lists_hbm, lists_ref, small_sem.at[1]),
        pltpu.make_async_copy(tmpl_hbm, tmpl_v, small_sem.at[2]),
    ]
    for copy in small:
        copy.start()
    loads = []
    for k in range(CHUNKS):
        cols = slice(k * per_chunk * LANES, (k + 1) * per_chunk * LANES)
        loads.append(pltpu.make_async_copy(wave_ref.at[:, cols], wave_v.at[:, cols], wave_sem.at[k]))
        loads[-1].start()
    for copy in small:
        copy.wait()
    for c in range(channels):
        flat[c * members : (c + 1) * members, :] = tmpl_v[c].astype(jnp.float32)
    if padded_rows > members * channels:
        flat[members * channels :, :] = jnp.zeros((padded_rows - members * channels, window_len), jnp.float32)
    gathered[me] = flat[...].astype(jnp.bfloat16)

    base = region * rows

    def pick(first, last):
        def body(which, carry):
            owner = owner_ref[which // members]
            for c in range(channels):
                row = jnp.clip(lists_ref[owner, lax.rem(which, members), c] - base, 0, rows - 1)
                at = which * channels + c
                for j in range(first, last):
                    value = wide[j, pl.ds(row, 1), :]
                    picked[at, j : j + 1, :] = value
                    if j < reach:
                        head[j, pl.ds(at, 1), :] = value
            return carry

        lax.fori_loop(0, total, body, 0)

    rim_copy = pltpu.make_async_remote_copy(
        src_ref=head_out, dst_ref=rim_in, send_sem=rim_send, recv_sem=rim_recv,
        device_id=(region, lax.rem(me + count - 1, count)), device_id_type=MESH)
    sent = []
    for k in range(CHUNKS):
        loads[k].wait()
        for j in range(k * per_chunk, (k + 1) * per_chunk):
            wide[j] = wave_v[:, LANES * j : LANES * (j + 1)].astype(jnp.float32)
        pick(k * per_chunk, (k + 1) * per_chunk)
        if k == EARLY - 1:
            head_out[...] = head[...].astype(jnp.bfloat16)
            pl.semaphore_wait(barrier, count + regions - 2)
            rim_copy.start()
            for d in range(1, count):
                sent.append(pltpu.make_async_remote_copy(
                    src_ref=gathered.at[me], dst_ref=gathered.at[me],
                    send_sem=block_send.at[d], recv_sem=block_recv.at[d],
                    device_id=(region, lax.rem(me + d, count)), device_id_type=MESH))
                sent[-1].start()

    sub = lax.broadcasted_iota(jnp.int32, (LANES, LANES), 0)
    lane = lax.broadcasted_iota(jnp.int32, (LANES, LANES), 1)
    upper = lane >= sub
    ones = jnp.ones((LANES, LANES), jnp.bfloat16)
    zeros = jnp.zeros((LANES, LANES), jnp.bfloat16)
    band = jnp.concatenate(
        [jnp.where(upper, ones, zeros)] + [ones] * (reach - 1) + [jnp.where(upper, zeros, ones)], axis=1
    )

    rim_copy.wait()
    inner = (me < count - 1).astype(jnp.float32)
    rim[...] = rim_in[...].astype(jnp.float32) * inner

    def window_sums(which, carry):
        stacked = []
        for c in range(channels):
            at = which * channels + c
            for j in range(reach):
                picked[at, blocks + j : blocks + j + 1, :] = rim[j, pl.ds(at, 1), :]
            pieces = [picked[at, j : j + blocks, :] for j in range(reach + 1)]
            squares = [p * p for p in pieces]
            high = [s.astype(jnp.bfloat16) for s in squares]
            low = [(s - h.astype(jnp.float32)).astype(jnp.bfloat16) for s, h in zip(squares, high)]
            record = jnp.concatenate([p.astype(jnp.bfloat16) for p in pieces], axis=1)
            series[at] = record
            stacked += [record, jnp.concatenate(high, axis=1), jnp.concatenate(low, axis=1)]
        sums = lax.dot_general(
            jnp.concatenate(stacked, axis=0), band, NT_DIMS, preferred_element_type=jnp.float32
        ).reshape(channels, 3, blocks, LANES)
        mean = sums[:, 0] / window_len
        spread = (sums[:, 1] + sums[:, 2]) / window_len - mean * mean
        inverse[pl.ds(which * channels, channels)] = lax.rsqrt(window_len * (spread + 1e-05))
        return carry

    lax.fori_loop(0, total, window_sums, 0)

    for d in range(1, count):
        source = lax.rem(me + count - d, count)
        pltpu.make_async_remote_copy(
            src_ref=gathered.at[source], dst_ref=gathered.at[source], send_sem=block_send.at[d], recv_sem=block_recv.at[d],
            device_id=(region, source), device_id_type=MESH).wait_recv()
    for r in range(rounds):
        unit = unit_rows(gathered[owner_ref[r]].astype(jnp.float32)).astype(jnp.float32)
        for j in range(reach):
            units[j, r * padded_rows : (r + 1) * padded_rows, :] = unit[:, LANES * j : LANES * (j + 1)]

    def scores(which):
        total_value = jnp.zeros((blocks, LANES), jnp.float32)
        first = which // members * padded_rows + lax.rem(which, members)
        for c in range(channels):
            pieces = [units[j, pl.ds(first + c * members, 1), :] for j in range(reach)]
            numer = lax.dot_general(
                series[which * channels + c], shifted_rows(pieces, upper), NT_DIMS,
                preferred_element_type=jnp.float32)
            total_value += numer * inverse[which * channels + c]
        acc[which] = total_value

    parts = []
    for k in range(regions):
        quarter = lax.rem(region + 1 + k, regions)

        def body(i, carry):
            scores(quarter * share + i)
            return carry

        lax.fori_loop(0, share, body, 0)
        if k < regions - 1:
            parts.append(pltpu.make_async_remote_copy(
                src_ref=acc.at[pl.ds(quarter * share, share)], dst_ref=part.at[k],
                send_sem=part_send.at[k], recv_sem=part_recv.at[k],
                device_id=(quarter, me), device_id_type=MESH))
            parts[-1].start()

    own = pl.ds(region * share, share)
    value = acc[own]
    for k in range(regions - 1):
        parts[k].wait_recv()
        value += part[k]
    res[own] = value.astype(jnp.bfloat16)
    results = []
    for d in range(1, regions):
        results.append(pltpu.make_async_remote_copy(
            src_ref=res.at[own], dst_ref=res.at[own], send_sem=res_send.at[d], recv_sem=res_recv.at[d],
            device_id=(lax.rem(region + d, regions), me), device_id_type=MESH))
        results[-1].start()
    for d in range(1, regions):
        source = lax.rem(region + regions - d, regions)
        theirs = pl.ds(source * share, share)
        pltpu.make_async_remote_copy(
            src_ref=res.at[theirs], dst_ref=res.at[theirs], send_sem=res_send.at[d], recv_sem=res_recv.at[d],
            device_id=(source, me), device_id_type=MESH).wait_recv()
    for copy in sent + parts + results:
        copy.wait_send()
    acc[...] = res[...].astype(jnp.float32)
    for j in range(blocks):
        out_ref[:, LANES * j : LANES * (j + 1)] = acc[:, j, :]


def per_device(waveforms, templates, channel_lists, owner_ranks):
    members, channels, window_len = templates.shape[1:]
    region_rows, slab_len = waveforms.shape
    count = lax.axis_size("tm")
    regions = lax.axis_size("region")
    rounds = owner_ranks.shape[0]
    total = rounds * members
    pairs = total * channels
    blocks = slab_len // LANES
    reach = window_len // LANES
    padded_rows = -(-members * channels // 16) * 16
    share = total // regions
    vmem = pl.BlockSpec(memory_space=pltpu.VMEM)
    hbm = pl.BlockSpec(memory_space=pl.ANY)
    dma = pltpu.SemaphoreType.DMA

    def body(*refs):
        kernel(count, regions, members, channels, *refs)

    detection = pl.pallas_call(
        body,
        out_shape=jax.ShapeDtypeStruct((total, slab_len), jnp.float32),
        in_specs=[hbm] * 4,
        out_specs=vmem,
        scratch_shapes=[
            pltpu.SMEM(owner_ranks.shape, jnp.int32),
            pltpu.SMEM(channel_lists.shape, jnp.int32),
            pltpu.VMEM((channels, members, window_len), jnp.bfloat16),
            pltpu.VMEM((padded_rows, window_len), jnp.float32),
            dma((3,)),
            pltpu.VMEM((region_rows, slab_len), jnp.bfloat16),
            pltpu.VMEM((blocks, region_rows, LANES), jnp.float32),
            pltpu.VMEM((pairs, blocks + reach, LANES), jnp.float32),
            pltpu.VMEM((reach, pairs, LANES), jnp.float32),
            pltpu.VMEM((reach, pairs, LANES), jnp.bfloat16),
            pltpu.VMEM((reach, pairs, LANES), jnp.bfloat16),
            pltpu.VMEM((reach, pairs, LANES), jnp.float32),
            pltpu.VMEM((count, padded_rows, window_len), jnp.bfloat16),
            pltpu.VMEM((reach, rounds * padded_rows, LANES), jnp.float32),
            pltpu.VMEM((pairs, blocks, LANES + window_len), jnp.bfloat16),
            pltpu.VMEM((pairs, blocks, LANES), jnp.float32),
            pltpu.VMEM((total, blocks, LANES), jnp.float32),
            pltpu.VMEM((regions - 1, share, blocks, LANES), jnp.float32),
            pltpu.VMEM((total, blocks, LANES), jnp.bfloat16),
            dma((CHUNKS,)),
            dma((count,)),
            dma((count,)),
            dma,
            dma,
            dma((regions,)),
            dma((regions,)),
            dma((regions,)),
            dma((regions,)),
        ],
        compiler_params=pltpu.CompilerParams(
            vmem_limit_bytes=56 << 20, collective_id=0, has_side_effects=True
        ),
    )(owner_ranks, channel_lists, waveforms, templates[0].transpose(1, 0, 2))
    starts = lax.axis_index("tm") * slab_len + jnp.arange(slab_len, dtype=jnp.int32)
    return jnp.where((starts <= slab_len * count - window_len)[None, :], detection, jnp.float32(0.0))


def solution(mesh):
    placed = (P("region", "tm"), P("tm", None, "region", None), P(None, None, "region"), P())
    return jax.shard_map(
        per_device, mesh=mesh, in_specs=placed, out_specs=P(None, "tm"), check_vma=False
    )
```
